32 devices in a mesh: grp: 2 (over x), samp: 4 (over y, core), col: 4 (over z).
Axes of the slice: x: 2, y: 2, z: 4, core: 2. Of those that a mesh axis runs over, the one named last changes fastest.
Arguments:
- dosage: bfloat16 [2048, 20480], P('samp', 'col'), may hold values from -6 to 6
- candidates: bfloat16 [2048, 16384], P('samp', 'col'), may hold values from -6 to 6
- traits: float32 [32, 2048], P('grp', 'samp'), parts along dimension 0, may hold values from -6 to 6
- coef_start: float32 [32, 20480], P('grp', 'col'), parts along dimension 0, may hold values from -0.0390625 to 0.0390625
- screened: int32 [1024], replicated, may hold values from 0 to 16383, as said below
- penalty: float32 [32], P('grp'), parts along dimension 0, may hold values from 0.002 to 0.05
Outputs:
- residual: float32 [32, 2048], P('grp', 'samp'), parts along dimension 0
- score: float32 [32, 16384], P('grp', 'col'), parts along dimension 0
The draws below stay inside these ranges and needn't reach their ends.
There are 2 independent parts, one for each index of `grp`. The reference program is written for one: setup_inputs(seed, part) draws one part's arguments, and reference() takes and returns one part's arrays. A program takes and returns all parts, laid end to end along the dimension named above; an argument that names none is the same for every part. Nothing has to cross between parts.
Inputs may be any that keep to these rules, and one draw needn't show every extreme that they name: `screened`: entries are distinct. In each aligned block of 256 entries, at most 128 lie in one block of 4096 candidate indices, and exactly 128 in one such block.
All inputs are finite; a program needn't handle non-finite values.
Results may differ from the reference program's by a relative error of at most 0.008.
Values may be sent and summed in bfloat16 or wider, within the bound.
A program may use at most 64 MiB of HBM per device.

```python
import math
import jax
import jax.numpy as jnp
from jax import lax

TRAITS = 16
NEW_DEV = 256
MOST = 128
CAND_DEV = 4096
ITERS = 2
SAMPLES = 2048
ACTIVE = 20480
NEW = 1024
CAND = 16384


def draw_screened(key, part):
    key = jax.random.fold_in(key, 11)
    block_count = NEW // NEW_DEV
    source_count = CAND // CAND_DEV
    key_heavy, key_order, key_local = jax.random.split(key, 3)
    heavy = jax.random.randint(key_heavy, (block_count,), 0, source_count)
    positions = jnp.arange(NEW_DEV)
    spread = (positions - MOST) % (source_count - 1)
    others = (heavy[:, None] + 1 + spread[None, :]) % source_count
    block_src = jnp.where(positions[None, :] < MOST, heavy[:, None], others)
    order_keys = jax.random.split(key_order, block_count)
    shuffles = jax.vmap(lambda part_key: jax.random.permutation(part_key, NEW_DEV))(order_keys)
    block_src = jnp.take_along_axis(block_src, shuffles, axis=1)
    source = block_src.reshape(-1)
    one_hot = (source[:, None] == jnp.arange(source_count)[None, :]).astype(jnp.int32)
    slot_rank = jnp.sum(jnp.cumsum(one_hot, axis=0) * one_hot, axis=1) - 1
    local_keys = jax.random.split(key_local, source_count)
    local_perms = jax.vmap(lambda part_key: jax.random.permutation(part_key, CAND_DEV))(local_keys)
    local_index = local_perms[source, slot_rank]
    return (source * CAND_DEV + local_index).astype(jnp.int32)


def block_levels(key, extent, cuts, low, top_value):
    factor_of, own = 1.0, jax.random.fold_in(key, 6)
    for axis_at, blocks in cuts:
        steps = jnp.exp(jax.random.uniform(jax.random.fold_in(own, axis_at), (blocks,), jnp.float32, low / len(cuts), top_value / len(cuts)))
        factor_of = factor_of * jnp.repeat(steps, extent[axis_at] // blocks).reshape([-1 if axis == axis_at else 1 for axis in range(len(extent))])
    return factor_of


def scatter_about(key, dims, scale, limit, cuts=(), kind=jnp.bfloat16):
    gain = block_levels(key, dims, cuts, -0.22, 0.18) if cuts else 1.0
    entries = jax.random.normal(key, dims, jnp.float32) * scale * gain
    return jnp.minimum(jnp.maximum(entries, -limit), limit).astype(kind)


def setup_inputs(seed: int = 0, part: int = 0) -> dict:
    seeds = jax.random.split(jax.random.key(seed), 7)
    own_keys = jax.random.split(jax.random.fold_in(seeds[6], part), 7)
    dosage = scatter_about(seeds[0], (SAMPLES, ACTIVE), 1.0, 6.0, ((0, 4), (1, 4)))
    candidates = scatter_about(seeds[1], (SAMPLES, CAND), 1.0, 6.0, ((0, 4), (1, 4)))
    traits = scatter_about(own_keys[2], (TRAITS, SAMPLES), 1.0, 6.0, ((1, 4),), jnp.float32)
    coef_start = scatter_about(own_keys[3], (TRAITS, ACTIVE), ACTIVE ** -0.5, 0.0390625, ((1, 4),), jnp.float32)
    screened = draw_screened(jax.random.fold_in(seeds[6], 71), part)
    penalty = jnp.clip(jnp.exp(jax.random.uniform(own_keys[5], (TRAITS,), jnp.float32, math.log(0.002), math.log(0.05))), 0.002, 0.05)
    return dict(dosage=dosage, candidates=candidates, traits=traits, coef_start=coef_start, screened=screened, penalty=penalty)


def rows_dot(left, right):
    return lax.dot_general(left, right, (((1,), (1,)), ((), ())), preferred_element_type=jnp.float32)

def fitted_values(coef_now, dosage, admitted):
    coef_bf = coef_now.astype(jnp.bfloat16)
    return rows_dot(coef_bf[:, :ACTIVE], dosage) + rows_dot(coef_bf[:, ACTIVE:], admitted)

def reference(dosage, candidates, traits, coef_start, screened, penalty):
    admitted = jnp.take(candidates, screened.astype(jnp.int32), axis=1)
    step_size = 1.0 / (1.0 + math.sqrt((ACTIVE + NEW) / SAMPLES)) ** 2
    threshold = (step_size * penalty)[:, None]
    coef_now = jnp.concatenate([coef_start, jnp.zeros((TRAITS, NEW), jnp.float32)], axis=1)
    for sweep in range(ITERS):
        fitted = fitted_values(coef_now, dosage, admitted)
        resid_bf = (traits - fitted).astype(jnp.bfloat16)
        gradient = jnp.concatenate([jnp.dot(resid_bf, dosage, preferred_element_type=jnp.float32), jnp.dot(resid_bf, admitted, preferred_element_type=jnp.float32)], axis=1) / SAMPLES
        moved = coef_now + step_size * gradient
        coef_now = moved - jnp.clip(moved, -threshold, threshold)
    residual = traits - fitted_values(coef_now, dosage, admitted)
    resid_bf = residual.astype(jnp.bfloat16)
    score = jnp.dot(resid_bf, candidates, preferred_element_type=jnp.float32) / math.sqrt(SAMPLES)
    return (residual, score)
```

```python
import functools
import math

import jax
import jax.numpy as jnp
from jax import lax
from jax.experimental import pallas as pl
from jax.experimental.pallas import tpu as pltpu
from jax.sharding import PartitionSpec as P

NEW_DEV = 256
MOST = 128
CAND_DEV = 4096
ITERS = 2
WIDE = 1024
LAG_A, LAG_B, LAG_C = 2, 4, 6

F32, BF16 = jnp.float32, jnp.bfloat16


def dot_nn(left, right):
    return jnp.dot(left, right, preferred_element_type=F32)


def dot_nt(left, right):
    return lax.dot_general(left, right, (((1,), (1,)), ((), ())), preferred_element_type=F32)


def kernel(
    sizes,
    dosage_hbm, cand_hbm, traits_hbm, coef_hbm, screened_hbm, penalty_hbm,
    resid_out, score_out,
    dosage, cand, traits, coef_start, screened, penalty,
    one_hot, admitted, coef_new, resid_f32, resid_bf, score_half,
    fit_slots, grad_bf, from_core, chip_sums, coef_bf,
    load_sem, cand_sem, small_sem, out_sem,
    fit_send, fit_recv, a_send, a_recv, b_send, b_recv, c_send, c_recv,
):
    n_col, n_samp, samples, step_size = sizes
    n_y = n_samp // 2
    col = lax.axis_index("col")
    samp = lax.axis_index("samp")
    core = lax.rem(samp, 2)
    other = 1 - core
    y_at = lax.div(samp, 2)
    core_peer = {"samp": y_at * 2 + other}
    y_peers = [{"samp": lax.rem(y_at + d, n_y) * 2 + core} for d in range(1, n_y)]
    col_peers = [{"col": lax.rem(col + d, n_col)} for d in range(1, n_col)]

    active = dosage.shape[1]
    slots = admitted.shape[1]
    n_dos = active // WIDE
    n_cand = CAND_DEV // WIDE

    loads = []
    for i in range(n_dos):
        at = (slice(None), pl.ds(i * WIDE, WIDE))
        loads.append(pltpu.make_async_copy(dosage_hbm.at[at], dosage.at[at], load_sem.at[i]))
    small = [
        pltpu.make_async_copy(src, dst, small_sem.at[i])
        for i, (src, dst) in enumerate(
            [(coef_hbm, coef_start), (traits_hbm, traits), (screened_hbm, screened), (penalty_hbm, penalty)]
        )
    ]
    cand_load = pltpu.make_async_copy(cand_hbm, cand, cand_sem.at[0])
    small[0].start()
    for copy in loads:
        copy.start()
    for copy in small[1:]:
        copy.start()
    cand_load.start()

    barrier = pltpu.get_barrier_semaphore()
    for peer in [core_peer] + y_peers + col_peers:
        pl.semaphore_signal(barrier, inc=1, device_id=peer, device_id_type=pl.DeviceIdType.MESH)

    sends = []

    def remote(src, dst, send_sem, recv_sem, peer):
        copy = pltpu.make_async_remote_copy(
            src_ref=src, dst_ref=dst, send_sem=send_sem, recv_sem=recv_sem,
            device_id=peer, device_id_type=pl.DeviceIdType.MESH,
        )
        copy.start()
        sends.append(copy)
        return copy

    def send_fit(turn, fitted):
        fit_slots[turn, col] = fitted.astype(BF16)
        return [
            remote(
                fit_slots.at[turn, col], fit_slots.at[turn, col],
                fit_send.at[turn, d], fit_recv.at[turn, d], peer,
            )
            for d, peer in enumerate(col_peers)
        ]

    def take_fit(turn, copies):
        for copy in copies:
            copy.wait_recv()
        total = fit_slots[turn, 0].astype(F32)
        for c in range(1, n_col):
            total = total + fit_slots[turn, c].astype(F32)
        resid_f32[...] = traits[...] - total
        resid_bf[...] = resid_f32[...].astype(BF16)

    small[0].wait()
    fitted = jnp.zeros(traits.shape, F32)
    for i in range(n_dos):
        loads[i].wait()
        at = slice(i * WIDE, (i + 1) * WIDE)
        fitted = fitted + dot_nt(coef_start[:, at].astype(BF16), dosage[:, at])
    pl.semaphore_wait(barrier, 1 + len(y_peers) + len(col_peers))
    fit_copies = send_fit(0, fitted)

    for copy in small[1:]:
        copy.wait()
    names = screened[...]
    local = names - col * CAND_DEV
    owned = (local >= 0) & (local < CAND_DEV)
    owned_f = jnp.where(owned, 1.0, 0.0)
    upper = (
        lax.broadcasted_iota(jnp.int32, (NEW_DEV, NEW_DEV), 0)
        <= lax.broadcasted_iota(jnp.int32, (NEW_DEV, NEW_DEV), 1)
    )
    rank = dot_nn(owned_f.astype(BF16), jnp.where(upper, 1.0, 0.0).astype(BF16)) * owned_f
    want = lax.broadcasted_iota(jnp.int32, (MOST, NEW_DEV), 0).astype(F32) + 1.0
    lanes = lax.broadcasted_iota(jnp.int32, (MOST, WIDE), 1).astype(F32)
    local_f = local.astype(F32) + 1.0
    for b in range(n_col):
        hit = rank[b : b + 1, :] == want
        column = jnp.sum(jnp.where(hit, local_f[b : b + 1, :], 0.0), axis=1, keepdims=True) - 1.0
        for i in range(n_cand):
            one_hot[b * MOST : (b + 1) * MOST, i * WIDE : (i + 1) * WIDE] = jnp.where(
                lanes == column - float(i * WIDE), 1.0, 0.0
            ).astype(BF16)
    cand_load.wait()
    for j in range(slots // 256):
        at = slice(j * 256, (j + 1) * 256)
        admitted[:, at] = dot_nt(cand[...], one_hot[at, :]).astype(BF16)

    threshold = step_size * penalty[...]
    scale = step_size / samples
    design = [(dosage, i * WIDE, WIDE) for i in range(n_dos)] + [(admitted, 0, slots)]
    tested = [(cand, i * WIDE, WIDE) for i in range(n_cand)]

    take_fit(0, fit_copies)

    for turn in range(ITERS + 1):
        last = turn == ITERS
        chunks = tested if last else design
        count = len(chunks)
        a_copies, b_copies, c_copies = {}, {}, {}
        fitted = jnp.zeros(traits.shape, F32)
        if last:
            out_copy = pltpu.make_async_copy(resid_f32, resid_out, out_sem.at[0])
            out_copy.start()
        outs = []
        resid = resid_bf[...]
        for t in range(count + LAG_C):
            if t < count:
                ref, start, width = chunks[t]
                half = width // 2
                part = dot_nn(resid, ref[:, start : start + width]).astype(BF16)
                grad_bf[turn, t, 0, :, :half] = part[:, :half]
                grad_bf[turn, t, 1, :, :half] = part[:, half:]
                a_copies[t] = remote(
                    grad_bf.at[turn, t, other, :, pl.ds(0, half)],
                    from_core.at[turn, t, :, pl.ds(0, half)],
                    a_send.at[turn, t], a_recv.at[turn, t], core_peer,
                )
            i = t - LAG_A
            if 0 <= i < count:
                half = chunks[i][2] // 2
                a_copies[i].wait_recv()
                chip_sum = grad_bf[turn, i, core, :, :half].astype(F32) + from_core[
                    turn, i, :, :half
                ].astype(F32)
                chip_sums[turn, i, y_at, :, :half] = chip_sum.astype(BF16)
                here = chip_sums.at[turn, i, y_at, :, pl.ds(0, half)]
                b_copies[i] = [
                    remote(here, here, b_send.at[turn, i, d], b_recv.at[turn, i, d], peer)
                    for d, peer in enumerate(y_peers)
                ]
            i = t - LAG_B
            if 0 <= i < count:
                ref, start, width = chunks[i]
                half = width // 2
                for copy in b_copies[i]:
                    copy.wait_recv()
                total = chip_sums[turn, i, 0, :, :half].astype(F32)
                for y in range(1, n_y):
                    total = total + chip_sums[turn, i, y, :, :half].astype(F32)
                if last:
                    score_half[i] = total * (1.0 / math.sqrt(samples))
                    here = score_out.at[:, pl.ds(pl.multiple_of(start + core * half, 128), half)]
                    copy = pltpu.make_async_copy(score_half.at[i], here, out_sem.at[1 + i])
                    copy.start()
                    outs.append(copy)
                    c_copies[i] = remote(
                        score_half.at[i], here, c_send.at[turn, i], c_recv.at[turn, i], core_peer
                    )
                else:
                    if turn > 0:
                        before = coef_new[i, :, :half]
                    elif ref is admitted:
                        before = jnp.zeros((traits.shape[0], half), F32)
                    else:
                        before = coef_start[:, pl.ds(pl.multiple_of(start + core * half, 128), half)]
                    moved = before + scale * total
                    after = moved - jnp.clip(moved, -threshold, threshold)
                    coef_new[i, :, :half] = after
                    coef_bf[turn, i, core, :, :half] = after.astype(BF16)
                    here = coef_bf.at[turn, i, core, :, pl.ds(0, half)]
                    c_copies[i] = remote(here, here, c_send.at[turn, i], c_recv.at[turn, i], core_peer)
            i = t - LAG_C
            if 0 <= i < count:
                ref, start, width = chunks[i]
                half = width // 2
                c_copies[i].wait_recv()
                if not last:
                    fitted = fitted + dot_nt(coef_bf[turn, i, 0, :, :half], ref[:, start : start + half])
                    fitted = fitted + dot_nt(
                        coef_bf[turn, i, 1, :, :half], ref[:, start + half : start + width]
                    )
        if not last:
            take_fit(turn + 1, send_fit(turn + 1, fitted))

    out_copy.wait()
    for copy in outs:
        copy.wait()
    for copy in sends:
        copy.wait_send()


def on_device(dosage, candidates, traits, coef_start, screened, penalty):
    n_col = lax.axis_size("col")
    n_samp = lax.axis_size("samp")
    rows, active = dosage.shape
    n_traits = traits.shape[0]
    samples = rows * n_samp
    total_cols = (active + NEW_DEV) * n_col
    step_size = 1.0 / (1.0 + math.sqrt(total_cols / samples)) ** 2
    slots = MOST * n_col
    chunks = active // WIDE + 1
    half = max(WIDE, slots) // 2
    turns = ITERS + 1
    n_y = n_samp // 2
    any_spec = pl.BlockSpec(memory_space=pl.ANY)
    dma = pltpu.SemaphoreType.DMA
    return pl.pallas_call(
        functools.partial(kernel, (n_col, n_samp, samples, step_size)),
        out_shape=(
            jax.ShapeDtypeStruct(traits.shape, F32),
            jax.ShapeDtypeStruct((n_traits, CAND_DEV), F32),
        ),
        in_specs=[any_spec] * 6,
        out_specs=(any_spec, any_spec),
        scratch_shapes=[
            pltpu.VMEM(dosage.shape, BF16),
            pltpu.VMEM(candidates.shape, BF16),
            pltpu.VMEM(traits.shape, F32),
            pltpu.VMEM(coef_start.shape, F32),
            pltpu.VMEM((n_col, NEW_DEV), jnp.int32),
            pltpu.VMEM((n_traits, 1), F32),
            pltpu.VMEM((slots, CAND_DEV), BF16),
            pltpu.VMEM((rows, slots), BF16),
            pltpu.VMEM((chunks, n_traits, half), F32),
            pltpu.VMEM(traits.shape, F32),
            pltpu.VMEM(traits.shape, BF16),
            pltpu.VMEM((CAND_DEV // WIDE, n_traits, WIDE // 2), F32),
            pltpu.VMEM((turns, n_col) + traits.shape, BF16),
            pltpu.VMEM((turns, chunks, 2, n_traits, half), BF16),
            pltpu.VMEM((turns, chunks, n_traits, half), BF16),
            pltpu.VMEM((turns, chunks, n_y, n_traits, half), BF16),
            pltpu.VMEM((ITERS, chunks, 2, n_traits, half), BF16),
            dma((active // WIDE,)),
            dma((1,)),
            dma((4,)),
            dma((1 + CAND_DEV // WIDE,)),
            dma((turns, n_col - 1)),
            dma((turns, n_col - 1)),
            dma((turns, chunks)),
            dma((turns, chunks)),
            dma((turns, chunks, n_y - 1)),
            dma((turns, chunks, n_y - 1)),
            dma((turns, chunks)),
            dma((turns, chunks)),
        ],
        compiler_params=pltpu.CompilerParams(
            collective_id=0, has_side_effects=True, vmem_limit_bytes=50 * 1024 * 1024
        ),
    )(
        dosage, candidates, traits, coef_start,
        screened.reshape(n_col, NEW_DEV), penalty.reshape(n_traits, 1),
    )


def solution(mesh):
    placed = (P("samp", "col"), P("samp", "col"), P("grp", "samp"), P("grp", "col"), P(), P("grp"))
    return jax.shard_map(
        on_device,
        mesh=mesh,
        in_specs=placed,
        out_specs=(P("grp", "samp"), P("grp", "col")),
        check_vma=False,
    )
```

```python
import functools
import math

import jax
import jax.numpy as jnp
from jax import lax
from jax.experimental import pallas as pl
from jax.experimental.pallas import tpu as pltpu
from jax.sharding import PartitionSpec as P

NEW_DEV = 256
MOST = 128
CAND_DEV = 4096
ITERS = 2
WIDE = 1024

F32, BF16 = jnp.float32, jnp.bfloat16


def dot_nn(left, right):
    return jnp.dot(left, right, preferred_element_type=F32)


def dot_nt(left, right):
    return lax.dot_general(left, right, (((1,), (1,)), ((), ())), preferred_element_type=F32)


def kernel(
    sizes,
    dosage_hbm, cand_hbm, traits_hbm, coef_hbm, screened_hbm, penalty_hbm,
    resid_out, score_out,
    dosage, cand, traits, coef_start, screened, penalty,
    one_hot, admitted, coef_new, resid_f32, resid_bf, sent, score_half,
    fit_slots, grad_bf, from_core, chip_sums, coef_bf,
    load_sem, cand_sem, small_sem, out_sem,
    fit_send, fit_recv, a_send, a_recv, b_send, b_recv, c_send, c_recv,
):
    n_col, n_samp, samples, step_size = sizes
    n_y = n_samp // 2
    col = lax.axis_index("col")
    samp = lax.axis_index("samp")
    core = lax.rem(samp, 2)
    other = 1 - core
    y_at = lax.div(samp, 2)
    core_peer = {"samp": y_at * 2 + other}
    y_peers = [{"samp": lax.rem(y_at + d, n_y) * 2 + core} for d in range(1, n_y)]
    col_peers = [{"col": lax.rem(col + d, n_col)} for d in range(1, n_col)]

    active = dosage.shape[1]
    slots = admitted.shape[1]
    n_dos = active // WIDE
    n_cand = CAND_DEV // WIDE

    loads = []
    for i in range(n_dos):
        at = (slice(None), pl.ds(i * WIDE, WIDE))
        loads.append(pltpu.make_async_copy(dosage_hbm.at[at], dosage.at[at], load_sem.at[i]))
    small = [
        pltpu.make_async_copy(src, dst, small_sem.at[i])
        for i, (src, dst) in enumerate(
            [(coef_hbm, coef_start), (traits_hbm, traits), (screened_hbm, screened), (penalty_hbm, penalty)]
        )
    ]
    cand_load = pltpu.make_async_copy(cand_hbm, cand, cand_sem.at[0])
    small[0].start()
    for copy in loads:
        copy.start()
    for copy in small[1:]:
        copy.start()
    cand_load.start()

    barrier = pltpu.get_barrier_semaphore()
    for peer in [core_peer] + y_peers + col_peers:
        pl.semaphore_signal(barrier, inc=1, device_id=peer, device_id_type=pl.DeviceIdType.MESH)

    sends = []

    def remote(src, dst, send_sem, recv_sem, peer):
        copy = pltpu.make_async_remote_copy(
            src_ref=src, dst_ref=dst, send_sem=send_sem, recv_sem=recv_sem,
            device_id=peer, device_id_type=pl.DeviceIdType.MESH,
        )
        copy.start()
        sends.append(copy)
        return copy

    def send_fit(turn, fitted):
        change = (fitted if turn == 0 else fitted - sent[...]).astype(BF16)
        sent[...] = change.astype(F32) if turn == 0 else sent[...] + change.astype(F32)
        fit_slots[turn, col] = change
        return [
            remote(
                fit_slots.at[turn, col], fit_slots.at[turn, col],
                fit_send.at[turn, d], fit_recv.at[turn, d], peer,
            )
            for d, peer in enumerate(col_peers)
        ]

    def take_fit(turn, copies):
        for copy in copies:
            copy.wait_recv()
        total = fit_slots[turn, 0].astype(F32)
        for c in range(1, n_col):
            total = total + fit_slots[turn, c].astype(F32)
        resid = (traits if turn == 0 else resid_f32)[...] - total
        resid_f32[...] = resid
        resid_bf[...] = resid.astype(BF16)

    small[0].wait()
    fitted = jnp.zeros(traits.shape, F32)
    for i in range(n_dos):
        loads[i].wait()
        at = slice(i * WIDE, (i + 1) * WIDE)
        fitted = fitted + dot_nt(coef_start[:, at].astype(BF16), dosage[:, at])
    pl.semaphore_wait(barrier, 1 + len(y_peers) + len(col_peers))
    fit_copies = send_fit(0, fitted)

    for copy in small[1:]:
        copy.wait()
    names = jnp.concatenate(
        [screened[pl.ds(b * NEW_DEV, NEW_DEV)].reshape(1, NEW_DEV) for b in range(n_col)], axis=0
    )
    local = names - col * CAND_DEV
    owned = (local >= 0) & (local < CAND_DEV)
    owned_f = jnp.where(owned, 1.0, 0.0)
    upper = (
        lax.broadcasted_iota(jnp.int32, (NEW_DEV, NEW_DEV), 0)
        <= lax.broadcasted_iota(jnp.int32, (NEW_DEV, NEW_DEV), 1)
    )
    rank = dot_nn(owned_f.astype(BF16), jnp.where(upper, 1.0, 0.0).astype(BF16)) * owned_f
    want = lax.broadcasted_iota(jnp.int32, (MOST, NEW_DEV), 0).astype(F32) + 1.0
    lanes = lax.broadcasted_iota(jnp.int32, (MOST, WIDE), 1).astype(F32)
    local_f = local.astype(F32) + 1.0
    for b in range(n_col):
        hit = rank[b : b + 1, :] == want
        column = jnp.sum(jnp.where(hit, local_f[b : b + 1, :], 0.0), axis=1, keepdims=True) - 1.0
        for i in range(n_cand):
            one_hot[b * MOST : (b + 1) * MOST, i * WIDE : (i + 1) * WIDE] = jnp.where(
                lanes == column - float(i * WIDE), 1.0, 0.0
            ).astype(BF16)
    cand_load.wait()
    for j in range(slots // 256):
        at = slice(j * 256, (j + 1) * 256)
        admitted[:, at] = dot_nt(cand[...], one_hot[at, :]).astype(BF16)

    n_traits = traits.shape[0]
    same = lax.broadcasted_iota(jnp.int32, (n_traits, n_traits), 0) == lax.broadcasted_iota(
        jnp.int32, (n_traits, n_traits), 1
    )
    penalty_row = penalty[...].reshape(1, n_traits)
    threshold = step_size * jnp.sum(jnp.where(same, penalty_row, 0.0), axis=1, keepdims=True)
    scale = step_size / samples
    design = [(dosage, i * WIDE, WIDE) for i in range(n_dos)] + [(admitted, 0, slots)]
    tested = [(cand, i * WIDE, WIDE) for i in range(n_cand)]

    take_fit(0, fit_copies)

    for turn in range(ITERS + 1):
        last = turn == ITERS
        chunks = tested if last else design
        count = len(chunks)
        a_copies, b_copies, c_copies = {}, {}, {}
        fitted = jnp.zeros(traits.shape, F32)
        if last:
            out_copy = pltpu.make_async_copy(resid_f32, resid_out, out_sem.at[0])
            out_copy.start()
        outs = []
        resid = resid_bf[...]
        for t in range(count):
            ref, start, width = chunks[t]
            half = width // 2
            part = dot_nn(resid, ref[:, start : start + width]).astype(BF16)
            grad_bf[turn, t, 0, :, :half] = part[:, :half]
            grad_bf[turn, t, 1, :, :half] = part[:, half:]
            a_copies[t] = remote(
                grad_bf.at[turn, t, other, :, pl.ds(0, half)],
                from_core.at[turn, t, :, pl.ds(0, half)],
                a_send.at[turn, t], a_recv.at[turn, t], core_peer,
            )
        for i in range(count):
            half = chunks[i][2] // 2
            a_copies[i].wait_recv()
            chip_sum = grad_bf[turn, i, core, :, :half].astype(F32) + from_core[
                turn, i, :, :half
            ].astype(F32)
            chip_sums[turn, i, y_at, :, :half] = chip_sum.astype(BF16)
            here = chip_sums.at[turn, i, y_at, :, pl.ds(0, half)]
            b_copies[i] = [
                remote(here, here, b_send.at[turn, i, d], b_recv.at[turn, i, d], peer)
                for d, peer in enumerate(y_peers)
            ]
        for i in range(count):
            ref, start, width = chunks[i]
            half = width // 2
            for copy in b_copies[i]:
                copy.wait_recv()
            total = chip_sums[turn, i, 0, :, :half].astype(F32)
            for y in range(1, n_y):
                total = total + chip_sums[turn, i, y, :, :half].astype(F32)
            if last:
                score_half[i] = total * (1.0 / math.sqrt(samples))
                here = score_out.at[:, pl.ds(pl.multiple_of(start + core * half, 128), half)]
                copy = pltpu.make_async_copy(score_half.at[i], here, out_sem.at[1 + i])
                copy.start()
                outs.append(copy)
                c_copies[i] = remote(
                    score_half.at[i], here, c_send.at[turn, i], c_recv.at[turn, i], core_peer
                )
            else:
                if turn > 0:
                    before = coef_new[i, :, :half]
                elif ref is admitted:
                    before = jnp.zeros((traits.shape[0], half), F32)
                else:
                    before = coef_start[:, pl.ds(pl.multiple_of(start + core * half, 128), half)]
                moved = before + scale * total
                after = moved - jnp.clip(moved, -threshold, threshold)
                coef_new[i, :, :half] = after
                coef_bf[turn, i, core, :, :half] = after.astype(BF16)
                here = coef_bf.at[turn, i, core, :, pl.ds(0, half)]
                c_copies[i] = remote(here, here, c_send.at[turn, i], c_recv.at[turn, i], core_peer)
        for i in range(count):
            ref, start, width = chunks[i]
            half = width // 2
            c_copies[i].wait_recv()
            if not last:
                fitted = fitted + dot_nt(coef_bf[turn, i, 0, :, :half], ref[:, start : start + half])
                fitted = fitted + dot_nt(
                    coef_bf[turn, i, 1, :, :half], ref[:, start + half : start + width]
                )
        if not last:
            take_fit(turn + 1, send_fit(turn + 1, fitted))

    out_copy.wait()
    for copy in outs:
        copy.wait()
    for copy in sends:
        copy.wait_send()


def on_device(dosage, candidates, traits, coef_start, screened, penalty):
    n_col = lax.axis_size("col")
    n_samp = lax.axis_size("samp")
    rows, active = dosage.shape
    n_traits = traits.shape[0]
    samples = rows * n_samp
    total_cols = (active + NEW_DEV) * n_col
    step_size = 1.0 / (1.0 + math.sqrt(total_cols / samples)) ** 2
    slots = MOST * n_col
    chunks = active // WIDE + 1
    half = max(WIDE, slots) // 2
    turns = ITERS + 1
    n_y = n_samp // 2
    any_spec = pl.BlockSpec(memory_space=pl.ANY)
    hbm_spec = pl.BlockSpec(memory_space=pltpu.HBM)
    dma = pltpu.SemaphoreType.DMA
    return pl.pallas_call(
        functools.partial(kernel, (n_col, n_samp, samples, step_size)),
        out_shape=(
            jax.ShapeDtypeStruct(traits.shape, F32),
            jax.ShapeDtypeStruct((n_traits, CAND_DEV), F32),
        ),
        in_specs=[hbm_spec] * 6,
        out_specs=(any_spec, any_spec),
        scratch_shapes=[
            pltpu.VMEM(dosage.shape, BF16),
            pltpu.VMEM(candidates.shape, BF16),
            pltpu.VMEM(traits.shape, F32),
            pltpu.VMEM(coef_start.shape, F32),
            pltpu.VMEM(screened.shape, jnp.int32),
            pltpu.VMEM(penalty.shape, F32),
            pltpu.VMEM((slots, CAND_DEV), BF16),
            pltpu.VMEM((rows, slots), BF16),
            pltpu.VMEM((chunks, n_traits, half), F32),
            pltpu.VMEM(traits.shape, F32),
            pltpu.VMEM(traits.shape, BF16),
            pltpu.VMEM(traits.shape, F32),
            pltpu.VMEM((CAND_DEV // WIDE, n_traits, WIDE // 2), F32),
            pltpu.VMEM((turns, n_col) + traits.shape, BF16),
            pltpu.VMEM((turns, chunks, 2, n_traits, half), BF16),
            pltpu.VMEM((turns, chunks, n_traits, half), BF16),
            pltpu.VMEM((turns, chunks, n_y, n_traits, half), BF16),
            pltpu.VMEM((ITERS, chunks, 2, n_traits, half), BF16),
            dma((active // WIDE,)),
            dma((1,)),
            dma((4,)),
            dma((1 + CAND_DEV // WIDE,)),
            dma((turns, n_col - 1)),
            dma((turns, n_col - 1)),
            dma((turns, chunks)),
            dma((turns, chunks)),
            dma((turns, chunks, n_y - 1)),
            dma((turns, chunks, n_y - 1)),
            dma((turns, chunks)),
            dma((turns, chunks)),
        ],
        compiler_params=pltpu.CompilerParams(
            collective_id=0, has_side_effects=True, vmem_limit_bytes=64 * 1024 * 1024
        ),
    )(
        dosage, candidates, traits, coef_start, screened, penalty
    )


def solution(mesh):
    placed = (P("samp", "col"), P("samp", "col"), P("grp", "samp"), P("grp", "col"), P(), P("grp"))
    return jax.shard_map(
        on_device,
        mesh=mesh,
        in_specs=placed,
        out_specs=(P("grp", "samp"), P("grp", "col")),
        check_vma=False,
    )
```

```python
import functools
import math

import jax
import jax.numpy as jnp
from jax import lax
from jax.experimental import pallas as pl
from jax.experimental.pallas import tpu as pltpu
from jax.sharding import PartitionSpec as P

NEW_DEV = 256
MOST = 128
CAND_DEV = 4096
ITERS = 2
WIDE = 1024

F32, BF16 = jnp.float32, jnp.bfloat16


def dot_nn(left, right):
    return jnp.dot(left, right, preferred_element_type=F32)


def dot_nt(left, right):
    return lax.dot_general(left, right, (((1,), (1,)), ((), ())), preferred_element_type=F32)


def kernel(
    sizes,
    dosage_hbm, cand_hbm, traits_hbm, coef_hbm, screened_hbm, penalty_hbm,
    resid_out, score_out,
    dosage, cand, traits, coef_start, screened, penalty,
    one_hot, admitted, coef_new, resid_f32, resid_bf, sent,
    fit_slots, grad_bf, from_core, chip_sums, coef_bf,
    load_sem, cand_sem, small_sem,
    fit_send, fit_recv, a_send, a_recv, b_send, b_recv, c_send, c_recv,
):
    n_col, n_samp, samples, step_size = sizes
    n_y = n_samp // 2
    col = lax.axis_index("col")
    samp = lax.axis_index("samp")
    core = lax.rem(samp, 2)
    other = 1 - core
    y_at = lax.div(samp, 2)
    core_peer = {"samp": y_at * 2 + other}
    y_peers = [{"samp": lax.rem(y_at + d, n_y) * 2 + core} for d in range(1, n_y)]
    col_peers = [{"col": lax.rem(col + d, n_col)} for d in range(1, n_col)]

    active = dosage.shape[1]
    slots = admitted.shape[1]
    n_dos = active // WIDE
    n_cand = CAND_DEV // WIDE

    loads = []
    for i in range(n_dos):
        at = (slice(None), pl.ds(i * WIDE, WIDE))
        loads.append(pltpu.make_async_copy(dosage_hbm.at[at], dosage.at[at], load_sem.at[i]))
    small = [
        pltpu.make_async_copy(src, dst, small_sem.at[i])
        for i, (src, dst) in enumerate(
            [(coef_hbm, coef_start), (traits_hbm, traits), (screened_hbm, screened), (penalty_hbm, penalty)]
        )
    ]
    cand_load = pltpu.make_async_copy(cand_hbm, cand, cand_sem.at[0])
    small[0].start()
    for copy in loads:
        copy.start()
    for copy in small[1:]:
        copy.start()
    cand_load.start()

    barrier = pltpu.get_barrier_semaphore()
    for peer in [core_peer] + y_peers + col_peers:
        pl.semaphore_signal(barrier, inc=1, device_id=peer, device_id_type=pl.DeviceIdType.MESH)

    sends = []

    def remote(src, dst, send_sem, recv_sem, peer):
        copy = pltpu.make_async_remote_copy(
            src_ref=src, dst_ref=dst, send_sem=send_sem, recv_sem=recv_sem,
            device_id=peer, device_id_type=pl.DeviceIdType.MESH,
        )
        copy.start()
        sends.append(copy)
        return copy

    def send_fit(turn, fitted):
        change = (fitted if turn == 0 else fitted - sent[...]).astype(BF16)
        sent[...] = change.astype(F32) if turn == 0 else sent[...] + change.astype(F32)
        fit_slots[turn, col] = change
        return [
            remote(
                fit_slots.at[turn, col], fit_slots.at[turn, col],
                fit_send.at[turn, d], fit_recv.at[turn, d], peer,
            )
            for d, peer in enumerate(col_peers)
        ]

    def take_fit(turn, copies):
        for copy in copies:
            copy.wait_recv()
        total = fit_slots[turn, 0].astype(F32)
        for c in range(1, n_col):
            total = total + fit_slots[turn, c].astype(F32)
        resid = (traits if turn == 0 else resid_f32)[...] - total
        resid_f32[...] = resid
        resid_bf[...] = resid.astype(BF16)

    small[0].wait()
    fitted = jnp.zeros(traits.shape, F32)
    for i in range(n_dos):
        loads[i].wait()
        at = slice(i * WIDE, (i + 1) * WIDE)
        fitted = fitted + dot_nt(coef_start[:, at].astype(BF16), dosage[:, at])
    pl.semaphore_wait(barrier, 1 + len(y_peers) + len(col_peers))
    fit_copies = send_fit(0, fitted)

    for copy in small[1:]:
        copy.wait()
    names = jnp.concatenate(
        [screened[pl.ds(b * NEW_DEV, NEW_DEV)].reshape(1, NEW_DEV) for b in range(n_col)], axis=0
    )
    local = names - col * CAND_DEV
    owned = (local >= 0) & (local < CAND_DEV)
    owned_f = jnp.where(owned, 1.0, 0.0)
    upper = (
        lax.broadcasted_iota(jnp.int32, (NEW_DEV, NEW_DEV), 0)
        <= lax.broadcasted_iota(jnp.int32, (NEW_DEV, NEW_DEV), 1)
    )
    rank = dot_nn(owned_f.astype(BF16), jnp.where(upper, 1.0, 0.0).astype(BF16)) * owned_f
    want = lax.broadcasted_iota(jnp.int32, (MOST, NEW_DEV), 0).astype(F32) + 1.0
    lanes = lax.broadcasted_iota(jnp.int32, (MOST, WIDE), 1).astype(F32)
    local_f = local.astype(F32) + 1.0
    for b in range(n_col):
        hit = rank[b : b + 1, :] == want
        column = jnp.sum(jnp.where(hit, local_f[b : b + 1, :], 0.0), axis=1, keepdims=True) - 1.0
        for i in range(n_cand):
            one_hot[b * MOST : (b + 1) * MOST, i * WIDE : (i + 1) * WIDE] = jnp.where(
                lanes == column - float(i * WIDE), 1.0, 0.0
            ).astype(BF16)
    cand_load.wait()
    for j in range(slots // 256):
        at = slice(j * 256, (j + 1) * 256)
        admitted[:, at] = dot_nt(cand[...], one_hot[at, :]).astype(BF16)

    n_traits = traits.shape[0]
    same = lax.broadcasted_iota(jnp.int32, (n_traits, n_traits), 0) == lax.broadcasted_iota(
        jnp.int32, (n_traits, n_traits), 1
    )
    penalty_row = penalty[...].reshape(1, n_traits)
    threshold = step_size * jnp.sum(jnp.where(same, penalty_row, 0.0), axis=1, keepdims=True)
    scale = step_size / samples
    design = [(dosage, i * WIDE, WIDE) for i in range(n_dos)] + [(admitted, 0, slots)]
    tested = [(cand, i * WIDE, WIDE) for i in range(n_cand)]

    take_fit(0, fit_copies)

    for turn in range(ITERS + 1):
        last = turn == ITERS
        chunks = tested if last else design
        count = len(chunks)
        a_copies, b_copies, c_copies = {}, {}, {}
        fitted = jnp.zeros(traits.shape, F32)
        if last:
            resid_out[...] = resid_f32[...]
        resid = resid_bf[...]
        for t in range(count):
            ref, start, width = chunks[t]
            half = width // 2
            part = dot_nn(resid, ref[:, start : start + width]).astype(BF16)
            grad_bf[turn, t, 0, :, :half] = part[:, :half]
            grad_bf[turn, t, 1, :, :half] = part[:, half:]
            a_copies[t] = remote(
                grad_bf.at[turn, t, other, :, pl.ds(0, half)],
                from_core.at[turn, t, :, pl.ds(0, half)],
                a_send.at[turn, t], a_recv.at[turn, t], core_peer,
            )
        for i in range(count):
            half = chunks[i][2] // 2
            a_copies[i].wait_recv()
            chip_sum = grad_bf[turn, i, core, :, :half].astype(F32) + from_core[
                turn, i, :, :half
            ].astype(F32)
            chip_sums[turn, i, y_at, :, :half] = chip_sum.astype(BF16)
            here = chip_sums.at[turn, i, y_at, :, pl.ds(0, half)]
            b_copies[i] = [
                remote(here, here, b_send.at[turn, i, d], b_recv.at[turn, i, d], peer)
                for d, peer in enumerate(y_peers)
            ]
        for i in range(count):
            ref, start, width = chunks[i]
            half = width // 2
            for copy in b_copies[i]:
                copy.wait_recv()
            total = chip_sums[turn, i, 0, :, :half].astype(F32)
            for y in range(1, n_y):
                total = total + chip_sums[turn, i, y, :, :half].astype(F32)
            if last:
                at = pl.ds(pl.multiple_of(start + core * half, 128), half)
                score_out[:, at] = total * (1.0 / math.sqrt(samples))
                here = score_out.at[:, at]
                c_copies[i] = remote(here, here, c_send.at[turn, i], c_recv.at[turn, i], core_peer)
            else:
                if turn > 0:
                    before = coef_new[i, :, :half]
                elif ref is admitted:
                    before = jnp.zeros((traits.shape[0], half), F32)
                else:
                    before = coef_start[:, pl.ds(pl.multiple_of(start + core * half, 128), half)]
                moved = before + scale * total
                after = moved - jnp.clip(moved, -threshold, threshold)
                coef_new[i, :, :half] = after
                coef_bf[turn, i, core, :, :half] = after.astype(BF16)
                here = coef_bf.at[turn, i, core, :, pl.ds(0, half)]
                c_copies[i] = remote(here, here, c_send.at[turn, i], c_recv.at[turn, i], core_peer)
        for i in range(count):
            ref, start, width = chunks[i]
            half = width // 2
            c_copies[i].wait_recv()
            if not last:
                fitted = fitted + dot_nt(coef_bf[turn, i, 0, :, :half], ref[:, start : start + half])
                fitted = fitted + dot_nt(
                    coef_bf[turn, i, 1, :, :half], ref[:, start + half : start + width]
                )
        if not last:
            take_fit(turn + 1, send_fit(turn + 1, fitted))

    for copy in sends:
        copy.wait_send()


def on_device(dosage, candidates, traits, coef_start, screened, penalty):
    n_col = lax.axis_size("col")
    n_samp = lax.axis_size("samp")
    rows, active = dosage.shape
    n_traits = traits.shape[0]
    samples = rows * n_samp
    total_cols = (active + NEW_DEV) * n_col
    step_size = 1.0 / (1.0 + math.sqrt(total_cols / samples)) ** 2
    slots = MOST * n_col
    chunks = active // WIDE + 1
    half = max(WIDE, slots) // 2
    turns = ITERS + 1
    n_y = n_samp // 2
    vmem_spec = pl.BlockSpec(memory_space=pltpu.VMEM)
    hbm_spec = pl.BlockSpec(memory_space=pltpu.HBM)
    dma = pltpu.SemaphoreType.DMA
    return pl.pallas_call(
        functools.partial(kernel, (n_col, n_samp, samples, step_size)),
        out_shape=(
            pltpu.VMEM(traits.shape, F32),
            pltpu.VMEM((n_traits, CAND_DEV), F32),
        ),
        in_specs=[hbm_spec] * 6,
        out_specs=(vmem_spec, vmem_spec),
        scratch_shapes=[
            pltpu.VMEM(dosage.shape, BF16),
            pltpu.VMEM(candidates.shape, BF16),
            pltpu.VMEM(traits.shape, F32),
            pltpu.VMEM(coef_start.shape, F32),
            pltpu.VMEM(screened.shape, jnp.int32),
            pltpu.VMEM(penalty.shape, F32),
            pltpu.VMEM((slots, CAND_DEV), BF16),
            pltpu.VMEM((rows, slots), BF16),
            pltpu.VMEM((chunks, n_traits, half), F32),
            pltpu.VMEM(traits.shape, F32),
            pltpu.VMEM(traits.shape, BF16),
            pltpu.VMEM(traits.shape, F32),
            pltpu.VMEM((turns, n_col) + traits.shape, BF16),
            pltpu.VMEM((turns, chunks, 2, n_traits, half), BF16),
            pltpu.VMEM((turns, chunks, n_traits, half), BF16),
            pltpu.VMEM((turns, chunks, n_y, n_traits, half), BF16),
            pltpu.VMEM((ITERS, chunks, 2, n_traits, half), BF16),
            dma((active // WIDE,)),
            dma((1,)),
            dma((4,)),
            dma((turns, n_col - 1)),
            dma((turns, n_col - 1)),
            dma((turns, chunks)),
            dma((turns, chunks)),
            dma((turns, chunks, n_y - 1)),
            dma((turns, chunks, n_y - 1)),
            dma((turns, chunks)),
            dma((turns, chunks)),
        ],
        compiler_params=pltpu.CompilerParams(
            collective_id=0, has_side_effects=True, vmem_limit_bytes=50 * 1024 * 1024
        ),
    )(
        *(
            pltpu.with_memory_space_constraint(arg, pltpu.HBM)
            for arg in (dosage, candidates, traits, coef_start, screened, penalty)
        )
    )


def solution(mesh):
    placed = (P("samp", "col"), P("samp", "col"), P("grp", "samp"), P("grp", "col"), P(), P("grp"))
    return jax.shard_map(
        on_device,
        mesh=mesh,
        in_specs=placed,
        out_specs=(P("grp", "samp"), P("grp", "col")),
        check_vma=False,
    )
```
